256 devices in a mesh: dp: 8 (over z_hi, core), expert: 32 (over x, y, z_lo).
Axes of the slice: x: 4, y: 4, z: 8 (z_hi: 4, z_lo: 2; z = z_hi * 2 + z_lo), core: 2. Of those that a mesh axis runs over, the one named last changes fastest.
Arguments:
- tokens: bfloat16 [16384, 2048], P(('dp', 'expert')), may hold values from -6 to 6
- out_grad: bfloat16 [16384, 2048], P(('dp', 'expert')), may hold values from -6 to 6
- expert_ids: int32 [16384, 8], P(('dp', 'expert')), may hold values from 0 to 63, as said below
- slot_positions: int32 [16384, 8], P(('dp', 'expert')), may hold values from 0 to 9, as said below
- keep_mask: int32 [16384, 8], P(('dp', 'expert')), may hold values from 0 to 1, as said below
- router_weight: bfloat16 [2048, 64], replicated, may hold values from -0.125 to 0.125
- w_gate: bfloat16 [64, 2048, 384], P('expert', 'dp'), may hold values from -0.125 to 0.125
- w_up: bfloat16 [64, 2048, 384], P('expert', 'dp'), may hold values from -0.125 to 0.125
- w_down: bfloat16 [64, 384, 2048], P('expert', None, 'dp'), may hold values from -0.3125 to 0.3125
Outputs:
- grad_tokens: bfloat16 [16384, 2048], P(('dp', 'expert'))
- grad_w_gate: bfloat16 [64, 2048, 384], P('expert', 'dp')
- grad_w_up: bfloat16 [64, 2048, 384], P('expert', 'dp')
- grad_w_down: bfloat16 [64, 384, 2048], P('expert', None, 'dp')
- grad_router: float32 [64, 2048], P('expert', 'dp')
The draws below stay inside these ranges and needn't reach their ends.
Inputs may be any that keep to these rules, and one draw needn't show every extreme that they name: `expert_ids`: each row names 8 different experts. `slot_positions`: within each block of 64 tokens, with choices taken in order of token and then of k, a choice's position is the number of earlier choices of the block that named the same expert; where that number is 10 or more the choice is dropped and its position is given as 9. Kept choices of one block never share an expert and a position. In every group of 32 blocks one expert has all 10 slots taken in every block. `keep_mask`: 1 exactly where the arrival count described for slot_positions is below 10; every block drops some choices.
All inputs are finite; a program needn't handle non-finite values.
Results may differ from the reference program's by a relative error of at most 0.027.
Values may be sent and summed in bfloat16 or wider, within the bound.
No kernel may reach another device: no remote copies, remote signals or barrier semaphores. Data moves between devices by JAX's collectives and lax.ppermute only.
A program may use at most 128 MiB of HBM per device.

```python
import jax
import jax.numpy as jnp
from jax import lax

D = 2048
F = 384
K = 8
TOK_DEV = 64
EXPERTS = 64
CAP = 10
GROUP_TOK = 2048
TOKENS = 16384
N_DP = 8


def routing_tables(key):
    base_key = jax.random.fold_in(key, 5)
    key_noise, key_hot, key_popular = jax.random.split(base_key, 3)
    block_count = TOKENS // TOK_DEV
    group_count = TOKENS // GROUP_TOK
    hot_expert = jax.random.randint(key_hot, (group_count,), 0, EXPERTS)
    popular = jax.random.randint(key_popular, (block_count, EXPERTS), 0, 4096)
    random_part = jax.random.randint(key_noise, (TOKENS, EXPERTS), 0, 8192)
    token_index = jnp.arange(TOKENS, dtype=jnp.int32)
    columns = jnp.arange(EXPERTS, dtype=jnp.int32)
    hot_column = (columns[None, :] == hot_expert[token_index // GROUP_TOK][:, None]).astype(jnp.int32)
    scoring = random_part + popular[token_index // TOK_DEV] + hot_column * 65536
    distinct = scoring * EXPERTS + columns[None, :]
    picked = lax.top_k(distinct, K)[1].astype(jnp.int32)
    onehot = (picked[:, :, None] == columns[None, None, :]).astype(jnp.int32)
    slot_flow = onehot.reshape(block_count, TOK_DEV * K, EXPERTS)
    before = jnp.cumsum(slot_flow, axis=1) - slot_flow
    arrival = jnp.sum(before * slot_flow, axis=2).reshape(TOKENS, K)
    kept_flag = (arrival < CAP).astype(jnp.int32)
    position = jnp.minimum(arrival, CAP - 1).astype(jnp.int32)
    return (picked, position, kept_flag)


def draw_expert_ids(key, part):
    return routing_tables(key)[0]


def draw_slot_positions(key, part):
    return routing_tables(key)[1]


def draw_keep_mask(key, part):
    return routing_tables(key)[2]


def block_levels(stream_key, extent, pieces, smallest, high):
    loudness, own = 1.0, jax.random.fold_in(stream_key, 6)
    for dim, blocks in pieces:
        heights = jnp.exp(jax.random.uniform(jax.random.fold_in(own, dim), (blocks,), jnp.float32, smallest / len(pieces), high / len(pieces)))
        loudness = loudness * jnp.repeat(heights, extent[dim] // blocks).reshape([-1 if axis == dim else 1 for axis in range(len(extent))])
    return loudness


def normal_values(key, dims, scale, reach, cuts=(), kind=jnp.bfloat16):
    gain = block_levels(key, dims, cuts, -0.22, 0.18) if cuts else 1.0
    values = jax.random.normal(key, dims, jnp.float32) * scale * gain
    return jnp.minimum(jnp.maximum(values, -reach), reach).astype(kind)


def setup_inputs(seed: int = 0) -> dict:
    streams_of = jax.random.split(jax.random.key(seed), 10)
    return {
        "tokens": normal_values(streams_of[0], (TOKENS, D), 1.0, 6.0, ((0, 256),)),
        "out_grad": normal_values(streams_of[1], (TOKENS, D), 1.0, 6.0, ((0, 256),)),
        "expert_ids": draw_expert_ids(jax.random.fold_in(streams_of[9], 71), 0),
        "slot_positions": draw_slot_positions(jax.random.fold_in(streams_of[9], 71), 0),
        "keep_mask": draw_keep_mask(jax.random.fold_in(streams_of[9], 71), 0),
        "router_weight": normal_values(streams_of[5], (D, EXPERTS), D ** -0.5, 0.125),
        "w_gate": normal_values(streams_of[6], (EXPERTS, D, F), D ** -0.5, 0.125, ((0, 32), (1, 8))),
        "w_up": normal_values(streams_of[7], (EXPERTS, D, F), D ** -0.5, 0.125, ((0, 32), (1, 8))),
        "w_down": normal_values(streams_of[8], (EXPERTS, F, D), F ** -0.5, 0.3125, ((0, 32), (2, 8))),
    }


def silu_parts(gate_pre):
    sigmoid_gate = jax.nn.sigmoid(gate_pre)
    return gate_pre * sigmoid_gate, sigmoid_gate * (1.0 + gate_pre * (1.0 - sigmoid_gate))


def routing_gates(tokens, expert_ids, router_weight):
    logits = jnp.dot(tokens, router_weight, preferred_element_type=jnp.float32)
    columns = jnp.arange(router_weight.shape[1], dtype=jnp.int32)
    chosen = expert_ids[:, :, None] == columns[None, None, :]
    picked = jnp.sum(jnp.where(chosen, logits[:, None, :], jnp.zeros((), logits.dtype)), axis=2)
    probits = jax.nn.sigmoid(picked)
    totals = jnp.sum(probits, axis=1, keepdims=True)
    return chosen, probits, totals, probits / totals


def router_backward(chosen, probits, totals, gate_share, taken_score):
    mean_score = jnp.sum(gate_share * taken_score, axis=1, keepdims=True)
    dlogit = (taken_score - mean_score) / totals * probits * (1.0 - probits)
    spread = jnp.where(chosen, dlogit[:, :, None], jnp.zeros((), dlogit.dtype))
    return jnp.sum(spread, axis=1).astype(jnp.bfloat16)


def expert_math(slot_tokens, slot_out_grad, slot_gate, gate_w, up_w, down_w):
    gate_pre = jnp.dot(slot_tokens, gate_w, preferred_element_type=jnp.float32)
    up_pre = jnp.dot(slot_tokens, up_w, preferred_element_type=jnp.float32)
    active, slope_term = silu_parts(gate_pre)
    hidden = (active * up_pre).astype(jnp.bfloat16)
    expert_out = jnp.dot(hidden, down_w, preferred_element_type=jnp.float32)
    score_rows = jnp.sum(expert_out * slot_out_grad.astype(jnp.float32), axis=1).astype(jnp.bfloat16)
    scaled = (slot_gate.astype(jnp.float32)[:, None] * slot_out_grad.astype(jnp.float32)).astype(jnp.bfloat16)
    hidden_grad = jnp.dot(scaled, down_w.T, preferred_element_type=jnp.float32)
    gate_grad = (hidden_grad * up_pre * slope_term).astype(jnp.bfloat16)
    up_grad = (hidden_grad * active).astype(jnp.bfloat16)
    input_grad = (jnp.dot(gate_grad, gate_w.T, preferred_element_type=jnp.float32)
                  + jnp.dot(up_grad, up_w.T, preferred_element_type=jnp.float32)).astype(jnp.bfloat16)
    return score_rows, scaled, hidden, gate_grad, up_grad, input_grad


def group_sum(left_rows, right_rows, pattern):
    row_count = left_rows.shape[0] // N_DP
    left_group = left_rows.reshape(N_DP, row_count, left_rows.shape[1]).astype(jnp.float32)
    right_group = right_rows.reshape(N_DP, row_count, right_rows.shape[1]).astype(jnp.float32)
    partials = jnp.einsum(pattern, left_group, right_group, precision=lax.Precision.HIGHEST)
    rounded = lax.optimization_barrier(partials.astype(jnp.bfloat16)).astype(jnp.float32)
    return jnp.sum(rounded, axis=0).astype(jnp.bfloat16)


def reference(tokens, out_grad, expert_ids, slot_positions, keep_mask, router_weight, w_gate, w_up, w_down):
    chosen, probits, totals, gate_share = routing_gates(tokens, expert_ids, router_weight)
    token_index = jnp.arange(TOKENS, dtype=jnp.int32)
    block_count = TOKENS // TOK_DEV
    slot_count = block_count * EXPERTS * CAP
    kept_flag = keep_mask > 0
    block_of = (token_index // TOK_DEV)[:, None]
    target = (block_of * EXPERTS + expert_ids) * CAP + slot_positions
    target = jnp.where(kept_flag, target, slot_count).reshape(-1).astype(jnp.int32)
    owners = jnp.broadcast_to(token_index[:, None], expert_ids.shape).reshape(-1)
    slot_owner = jnp.zeros((slot_count + 1,), jnp.int32).at[target].set(owners)[:slot_count]
    slot_live = jnp.zeros((slot_count + 1,), jnp.int32).at[target].set(jnp.ones_like(owners))[:slot_count]
    slot_weight = jnp.zeros((slot_count + 1,), jnp.float32).at[target].set(gate_share.reshape(-1))[:slot_count]
    slot_gate = slot_weight.astype(jnp.bfloat16)

    def per_expert(table):
        shaped = table.reshape(block_count, EXPERTS, CAP)
        return jnp.transpose(shaped, (1, 0, 2)).reshape(EXPERTS, block_count * CAP)

    owner_table = per_expert(slot_owner)
    live_table = per_expert(slot_live)
    gate_table = per_expert(slot_gate)

    def one_expert(grad_sum, inputs):
        owner_rows, live_rows, gate_rows, gate_w, up_w, down_w = inputs
        live_flag = (live_rows > 0)[:, None]
        slot_tokens = jnp.where(live_flag, tokens[owner_rows], jnp.zeros((), tokens.dtype))
        slot_out_grad = jnp.where(live_flag, out_grad[owner_rows], jnp.zeros((), out_grad.dtype))
        score_rows, scaled, hidden, gate_grad, up_grad, input_grad = expert_math(
            slot_tokens, slot_out_grad, gate_rows, gate_w, up_w, down_w)
        added = jnp.where(live_flag, input_grad.astype(jnp.float32), jnp.zeros((), jnp.float32))
        grad_sum = grad_sum.at[owner_rows].add(added)
        gate_wgrad = group_sum(slot_tokens, gate_grad, "grd,grf->gdf")
        up_wgrad = group_sum(slot_tokens, up_grad, "grd,grf->gdf")
        down_wgrad = group_sum(hidden, scaled, "grf,grd->gfd")
        return grad_sum, (score_rows, gate_wgrad, up_wgrad, down_wgrad)

    start_sum = jnp.zeros((TOKENS, D), jnp.float32)
    grad_sum, stacked = lax.scan(one_expert, start_sum,
                                 (owner_table, live_table, gate_table, w_gate, w_up, w_down))
    score_stack, grad_w_gate, grad_w_up, grad_w_down = stacked
    score_table = score_stack.reshape(EXPERTS, block_count, CAP)
    taken_score = score_table[expert_ids, block_of, slot_positions].astype(jnp.float32) * keep_mask.astype(jnp.float32)
    dlogits = router_backward(chosen, probits, totals, gate_share, taken_score)
    grad_tokens = (grad_sum + jnp.dot(dlogits, router_weight.T, preferred_element_type=jnp.float32)).astype(jnp.bfloat16)
    grad_router = jnp.dot(dlogits.T, tokens, preferred_element_type=jnp.float32)
    return grad_tokens, grad_w_gate, grad_w_up, grad_w_down, grad_router
```

```python
import jax
import jax.numpy as jnp
from jax import lax
from jax.experimental import pallas as pl
from jax.experimental.pallas import tpu as pltpu
from jax.sharding import Mesh
from jax.sharding import PartitionSpec as P

F32, BF16 = jnp.float32, jnp.bfloat16
AXES = ("zh", "core", "x", "y", "zl")
PLANE = ("x", "y")
CAP = 10
EXPERTS = 64
PLUS = [(i, (i + 1) % 4) for i in range(4)]
MINUS = [(i, (i + 3) % 4) for i in range(4)]
SWAP = [(0, 1), (1, 0)]


def mm(a, b, dims=((1,), (0,))):
    return lax.dot_general(a, b, (dims, ((), ())), preferred_element_type=F32)


def rolled(a, steps):
    q = a.shape[1] // 4
    out = a
    for i in range(1, 4):
        out = jnp.where(steps == i, jnp.concatenate([a[:, i * q :], a[:, : i * q]], axis=1), out)
    return out


def quad(a, other):
    pair = jnp.concatenate([a, other], axis=0)
    return jnp.concatenate([pair, lax.ppermute(pair, "core", SWAP)], axis=0)


def quad_sum(a):
    rows = a.shape[0] // 4
    a = a[: 2 * rows] + lax.ppermute(a[2 * rows :].astype(BF16), "core", SWAP).astype(F32)
    return a[:rows] + lax.ppermute(a[rows:].astype(BF16), "zl", SWAP).astype(F32)


def both_ways(up, down):
    return lax.ppermute(up, "zh", PLUS), lax.ppermute(down, "zh", MINUS)


def scatter_first(a):
    h = a.shape[0] // 8
    return both_ways(a[3 * h : 5 * h], a[5 * h : 7 * h])


def scatter_second(a, got_up, got_down):
    h = a.shape[0] // 8
    up = (a[2 * h : 3 * h].astype(F32) + got_up[h:].astype(F32)).astype(BF16)
    down = (a[7 * h :].astype(F32) + got_down[:h].astype(F32)).astype(BF16)
    return both_ways(*lax.optimization_barrier((up, down)))


def scatter_end(a, first, second):
    h = a.shape[0] // 8
    low = a[:h].astype(F32) + second[0].astype(F32) + first[1][h:].astype(F32)
    high = a[h : 2 * h].astype(F32) + first[0][:h].astype(F32) + second[1].astype(F32)
    return jnp.concatenate([low, high], axis=0).astype(BF16)


def a2a(a, axes):
    return lax.all_to_all(a, axes, split_axis=0, concat_axis=0, tiled=True)


def alone(ids, *arrays):
    return lax.cond(
        ids[0, 0] >= 0, lambda *v: tuple(a2a(w, PLANE) for w in v), lambda *v: v, *arrays
    )


def forward_kernel(x, s, own, after, far_lo, far_hi, prev, pre_grad, share, g_pre, g_down, hidden):
    hid = own.shape[1] // 3
    rows = x.shape[0] // 2
    pieces = []
    at = 0
    for w in (own, after, far_lo, far_hi, prev):
        pieces.append((w, at))
        at += w.shape[0]

    @pl.loop(0, 2)
    def _(i):
        tile = pl.ds(pl.multiple_of(i * rows, rows), rows)
        pre = jnp.zeros((rows, 2 * hid), F32)
        for w, at in pieces:
            pre += mm(x[tile, at : at + w.shape[0]], w[:, : 2 * hid])
        hgrad = jnp.zeros((rows, hid), F32)
        for w, at in pieces:
            hgrad += mm(s[tile, at : at + w.shape[0]], w[:, 2 * hid :])
        gate_pre, up_pre = pre[:, :hid], pre[:, hid:]
        sg = jax.nn.sigmoid(gate_pre)
        act = gate_pre * sg
        h = (act * up_pre).astype(BF16)
        hidden[tile, :] = h
        share[tile, :] = jnp.sum(h.astype(F32) * hgrad, axis=1, keepdims=True)
        slope = sg * (1.0 + gate_pre * (1.0 - sg))
        pre_grad[tile, :hid] = (hgrad * up_pre * slope).astype(BF16)
        pre_grad[tile, hid:] = (hgrad * act).astype(BF16)

    q = x.shape[1] // 4

    @pl.loop(0, 4)
    def _(j):
        cols = pl.ds(pl.multiple_of(j * q, q), q)
        g_pre[cols, :] = mm(x[:, cols], pre_grad[...], ((0,), (0,))).astype(BF16)
        g_down[cols, :] = mm(s[:, cols], hidden[...], ((0,), (0,))).astype(BF16)


def back_kernel(pre_grad, own, after, far_lo, far_hi, prev, back):
    hid = own.shape[1] // 3
    rows = pre_grad.shape[0] // 2

    @pl.loop(0, 2)
    def _(i):
        tile = pl.ds(pl.multiple_of(i * rows, rows), rows)
        at = 0
        for w in (own, after, far_lo, far_hi, prev):
            n = w.shape[0]
            back[tile, at : at + n] = mm(
                pre_grad[tile, :], w[:, : 2 * hid], ((1,), (1,))
            ).astype(BF16)
            at += n


def call(kernel, outs, scratch, *args):
    vmem = pl.BlockSpec(memory_space=pltpu.VMEM)
    return pl.pallas_call(
        kernel,
        out_shape=outs,
        in_specs=[vmem] * len(args),
        out_specs=[vmem] * len(outs),
        scratch_shapes=scratch,
        compiler_params=pltpu.CompilerParams(vmem_limit_bytes=48 * 2**20),
    )(*args)


def per_device(tokens, out_grad, ids, pos, keep, router, w_gate, w_up, w_down):
    tok, width = tokens.shape
    hid = w_gate.shape[2]
    piece = w_gate.shape[1]
    zh, core, zl = (lax.axis_index(n) for n in ("zh", "core", "zl"))
    chips = 16
    slots = chips * 4 * CAP

    experts = jnp.arange(EXPERTS, dtype=jnp.int32)
    hit = ids.T[None] == experts[:, None, None]
    chosen = jnp.any(hit, axis=1)
    held = hit & (keep.T > 0)[None]
    slot_t = (jnp.sum(jnp.where(held, pos.T[None] + 1, 0), axis=1) - 1).astype(BF16)
    logits = mm(router, tokens, ((0,), (1,)))
    sig = jax.nn.sigmoid(logits)
    prob = jnp.where(chosen, sig, 0.0)
    gate = prob / jnp.sum(prob, axis=0, keepdims=True)

    def mine(table):
        parts = table.reshape(chips, 4, table.shape[1])
        which = 2 * zl + core
        out = parts[:, 0]
        for i in range(1, 4):
            out = jnp.where(which == i, parts[:, i], out)
        return out

    zeros = jnp.zeros((tok, EXPERTS), BF16)
    tok_e = jnp.concatenate([rolled(tokens, zh), slot_t.T, zeros], axis=1)
    grad_e = jnp.concatenate([rolled(out_grad, zh), gate.astype(BF16).T, zeros], axis=1)
    tok_z, grad_z = (lax.ppermute(v, "zl", SWAP) for v in (tok_e, grad_e))
    shard = a2a(jnp.concatenate([w_gate, w_up, jnp.swapaxes(w_down, 1, 2)], axis=2), "core")
    shard, tok_z, grad_z = lax.optimization_barrier((shard, tok_z, grad_z))
    tok_q, grad_q = quad(tok_e, tok_z), quad(grad_e, grad_z)
    slot_q = mine(tok_q[:, width : width + EXPERTS].T)
    gate_q = mine(grad_q[:, width : width + EXPERTS].T)
    tok_q, grad_q = tok_q[:, :width], grad_q[:, :width]

    place = jnp.arange(4 * CAP, dtype=jnp.int32)
    block = jnp.arange(4 * tok, dtype=jnp.int32) // tok
    match = (slot_q.astype(jnp.int32)[:, None, :] == (place % CAP)[None, :, None]) & (
        (place // CAP)[:, None] == block[None, :]
    )
    pick = jnp.where(match, 1.0, 0.0).astype(BF16).reshape(slots, 4 * tok)
    pick_g = jnp.where(match, gate_q.astype(F32)[:, None, :], 0.0).astype(BF16).reshape(slots, 4 * tok)

    send_x = mm(pick, tok_q).astype(BF16).reshape(chips, 4 * CAP, width)
    send_s = mm(pick_g, grad_q).astype(BF16).reshape(chips, 4 * CAP, width)
    shard = shard.reshape(2 * piece, 3 * hid)
    after_before = both_ways(shard, shard)
    (x,) = alone(ids, send_x)
    x, send_s, (before, after) = lax.optimization_barrier((x, send_s, after_before))
    far = both_ways(before[:piece], after[piece:])
    (s,) = alone(ids, send_s)
    s, far = lax.optimization_barrier((s, far))
    x, s = x.reshape(slots, width), s.reshape(slots, width)
    weight = (shard, after, *far, before)

    of = jax.ShapeDtypeStruct
    pre_grad, share, g_pre, g_down = call(
        forward_kernel,
        (
            of((slots, 2 * hid), BF16),
            of((slots, 1), F32),
            of((width, 2 * hid), BF16),
            of((width, hid), BF16),
        ),
        [pltpu.VMEM((slots, hid), BF16)],
        x,
        s,
        *weight,
    )
    w_grads = g_pre, g_down

    share = share.reshape(chips, 2, 2, CAP)
    share = jnp.where(core == 0, share, share[:, ::-1])
    share = jnp.where(zl == 0, share, share[:, :, ::-1])
    share = jnp.swapaxes(share, 0, 1)
    share = a2a(share.reshape(64, 1, CAP), ("core", "x", "y", "zl"))
    share = share.reshape(2, 2 * chips, CAP).swapaxes(0, 1).reshape(EXPERTS, CAP)
    share, w_grads = lax.optimization_barrier((share, w_grads))
    firsts = [scatter_first(g) for g in w_grads]
    taken = jnp.zeros((EXPERTS, tok), F32)
    for i in range(CAP):
        taken += jnp.where(slot_t == i, share[:, i : i + 1], 0.0)
    mean = jnp.sum(taken, axis=0, keepdims=True)
    dlogits = jnp.where(chosen, (taken - gate * mean) * (1.0 - sig), 0.0).astype(BF16)
    term = mm(dlogits, tokens).astype(BF16).reshape(32, 2, width)
    own_part = mm(dlogits, router, ((0,), (1,)))

    (back,) = call(back_kernel, (of((slots, width), BF16),), [], pre_grad, *weight)
    back, term, own_part = lax.optimization_barrier((back, term, own_part))
    (back,) = alone(ids, back.reshape(chips, 4 * CAP, width))
    back, firsts, term = lax.optimization_barrier((back, firsts, term))
    seconds = [scatter_second(g, *f) for g, f in zip(w_grads, firsts)]
    part = quad_sum(mm(pick, back.reshape(slots, width), ((0,), (0,))))
    grad_tokens = (rolled(part, (4 - zh) % 4) + own_part).astype(BF16)
    term = jnp.sum(a2a(term, PLANE + ("zl",)).astype(F32), axis=0)
    term = term.reshape(2, 8, width // 8).swapaxes(0, 1)
    grad_router = jnp.sum(a2a(term, ("zh", "core")), axis=0)

    g_gate_up, g_down = (
        a2a(scatter_end(*g).reshape(2, piece, g[0].shape[1]), "core")
        for g in zip(w_grads, firsts, seconds)
    )
    return (
        grad_tokens,
        g_gate_up[:, :, :hid],
        g_gate_up[:, :, hid:],
        jnp.swapaxes(g_down, 1, 2),
        grad_router,
    )


def solution(mesh):
    grid = Mesh(mesh.devices.reshape(4, 2, 4, 4, 2), AXES)
    dp, ex = ("zh", "core"), ("x", "y", "zl")
    rows = P(AXES, None)
    return jax.shard_map(
        per_device,
        mesh=grid,
        in_specs=(rows,) * 5 + (P(), P(ex, dp, None), P(ex, dp, None), P(ex, None, dp)),
        out_specs=(rows, P(ex, dp, None), P(ex, dp, None), P(ex, None, dp), P(ex, dp)),
        check_vma=False,
    )
```

```python
import jax
import jax.numpy as jnp
from jax import lax
from jax.experimental import pallas as pl
from jax.experimental.pallas import tpu as pltpu
from jax.sharding import Mesh
from jax.sharding import PartitionSpec as P

F32, BF16 = jnp.float32, jnp.bfloat16
AXES = ("zh", "core", "x", "y", "zl")
PLANE = ("x", "y")
CAP = 10
EXPERTS = 64
PLUS = [(i, (i + 1) % 4) for i in range(4)]
MINUS = [(i, (i + 3) % 4) for i in range(4)]
OPPOSITE = [(i, (i + 2) % 4) for i in range(4)]
SWAP = [(0, 1), (1, 0)]


def mm(a, b, dims=((1,), (0,))):
    return lax.dot_general(a, b, (dims, ((), ())), preferred_element_type=F32)


def both_ways(up, down):
    return lax.ppermute(up, "zh", PLUS), lax.ppermute(down, "zh", MINUS)


def a2a(a, axes):
    return lax.all_to_all(a, axes, split_axis=0, concat_axis=0, tiled=True)


def alone(ids, *arrays):
    return lax.cond(
        ids[0, 0] >= 0, lambda *v: tuple(a2a(w, PLANE) for w in v), lambda *v: v, *arrays
    )


def at_unit(starts, unit, size):
    return pl.ds(pl.multiple_of(starts[unit], 256), size)


def forward_kernel(starts, x, s, own, after, far_lo, far_hi, prev, *refs):
    pre_out, spread, *outs = refs[:7]
    hidden, pre_grad, *grads, sems = refs[7:]
    hid = own.shape[1] // 3
    rows = x.shape[0] // 2
    pieces = ((own, 0), (after, 2), (far_lo, 4), (far_hi, 5), (prev, 6))

    @pl.loop(0, 2)
    def _(i):
        tile = pl.ds(pl.multiple_of(i * rows, rows), rows)
        pre = jnp.zeros((rows, 2 * hid), F32)
        for w, u in pieces:
            pre += mm(x[tile, at_unit(starts, u, w.shape[0])], w[:, : 2 * hid])
        hgrad = jnp.zeros((rows, hid), F32)
        for w, u in pieces:
            hgrad += mm(s[tile, at_unit(starts, u, w.shape[0])], w[:, 2 * hid :])
        gate_pre, up_pre = pre[:, :hid], pre[:, hid:]
        sg = jax.nn.sigmoid(gate_pre)
        act = gate_pre * sg
        h = (act * up_pre).astype(BF16)
        hidden[tile, :] = h
        share = jnp.sum(h.astype(F32) * hgrad, axis=1, keepdims=True)
        column = lax.broadcasted_iota(jnp.int32, (rows, spread.shape[1]), 1)
        spread[tile, :] = jnp.where(column == starts[8], share, 0.0)
        slope = sg * (1.0 + gate_pre * (1.0 - sg))
        pre_grad[tile, :hid] = (hgrad * up_pre * slope).astype(BF16)
        pre_grad[tile, hid:] = (hgrad * act).astype(BF16)

    copies = [pltpu.make_async_copy(pre_grad, pre_out, sems.at[len(outs)])]
    copies[0].start()
    firsts = (0, 2, 3, 5, 7)
    for k in (2, 3, 1, 4, 0):
        g = grads[k]
        for r in range(0, g.shape[0], 256):
            cols = at_unit(starts, firsts[k] + r // 256, 256)
            g[r : r + 256, : 2 * hid] = mm(x[:, cols], pre_grad[...], ((0,), (0,))).astype(BF16)
            g[r : r + 256, 2 * hid :] = mm(s[:, cols], hidden[...], ((0,), (0,))).astype(BF16)
        copies.append(pltpu.make_async_copy(g, outs[k], sems.at[k]))
        copies[-1].start()
    for copy in copies:
        copy.wait()


def back_kernel(starts, spread, pre_grad, own, after, far_lo, far_hi, prev, back):
    hid = own.shape[1] // 3
    rows = pre_grad.shape[0] // 2

    @pl.loop(0, 2)
    def _(i):
        tile = pl.ds(pl.multiple_of(i * rows, rows), rows)
        for w, u in ((own, 0), (after, 2), (far_lo, 4), (far_hi, 5), (prev, 6)):
            grad = mm(pre_grad[tile, :], w[:, : 2 * hid], ((1,), (1,)))
            back[tile, at_unit(starts, u, w.shape[0])] = grad.astype(BF16)
        back[tile, back.shape[1] - spread.shape[1] :] = spread[tile, :].astype(BF16)


def call(kernel, outs, spaces, scratch, *args):
    vmem = pl.BlockSpec(memory_space=pltpu.VMEM)
    smem = pl.BlockSpec(memory_space=pltpu.SMEM)
    return pl.pallas_call(
        kernel,
        out_shape=outs,
        in_specs=[smem if a.dtype == jnp.int32 else vmem for a in args],
        out_specs=[pl.BlockSpec(memory_space=space) for space in spaces],
        scratch_shapes=scratch,
        compiler_params=pltpu.CompilerParams(vmem_limit_bytes=40 * 2**20),
    )(*args)


def per_device(tokens, out_grad, ids, pos, keep, router, w_gate, w_up, w_down):
    tok, width = tokens.shape
    hid = w_gate.shape[2]
    piece = w_gate.shape[1]
    zh, core, zl = (lax.axis_index(n) for n in ("zh", "core", "zl"))
    chips = 16
    slots = chips * 4 * CAP

    experts = jnp.arange(EXPERTS, dtype=jnp.int32)
    hit = ids.T[None] == experts[:, None, None]
    chosen = jnp.any(hit, axis=1)
    held = hit & (keep.T > 0)[None]
    slot_t = (jnp.sum(jnp.where(held, pos.T[None] + 1, 0), axis=1) - 1).astype(BF16)
    logits = mm(router, tokens, ((0,), (1,)))
    sig = jax.nn.sigmoid(logits)
    prob = jnp.where(chosen, sig, 0.0)
    gate = prob / jnp.sum(prob, axis=0, keepdims=True)

    last = 2 * zl + core
    slot_c, gate_c = slot_t.T, gate.astype(BF16).T
    tok_e = jnp.concatenate([tokens, slot_c, jnp.zeros_like(gate_c)], axis=1)
    grad_e = jnp.concatenate([out_grad, slot_c, gate_c], axis=1)
    tok_z, grad_z = (lax.ppermute(v, "zl", SWAP) for v in (tok_e, grad_e))
    shard = a2a(jnp.concatenate([w_gate, w_up, jnp.swapaxes(w_down, 1, 2)], axis=2), "core")
    shard, tok_z, grad_z = lax.optimization_barrier((shard, tok_z, grad_z))
    shard = shard.reshape(2 * piece, 3 * hid)
    near = both_ways(shard, shard)
    far = [lax.ppermute(h, "zh", OPPOSITE) for h in (shard[:piece], shard[piece:])]

    def four(own, other):
        pair = jnp.concatenate([own, other], axis=0)
        return jnp.concatenate([pair, lax.ppermute(pair, "core", SWAP)], axis=0)

    every = 4 * jnp.arange(chips, dtype=jnp.int32) + last
    one = jnp.where(every[:, None] == experts[None, :], 1.0, 0.0).astype(BF16)

    def table(rows, at):
        return mm(one, rows[:, width + at : width + at + EXPERTS], ((1,), (1,)))

    place = jnp.arange(4 * CAP, dtype=jnp.int32)
    block = jnp.arange(4 * tok, dtype=jnp.int32) // tok
    same_block = (place // CAP)[:, None] == block[None, :]
    wanted = (place % CAP).astype(F32)[None, :, None]

    tok_q = four(tok_e, tok_z)
    grad_q = four(grad_e, grad_z)
    match = (table(tok_q, 0)[:, None, :] == wanted) & same_block
    pick = jnp.where(match, 1.0, 0.0).astype(BF16).reshape(slots, 4 * tok)
    pick_g = jnp.where(match, table(grad_q, EXPERTS)[:, None, :], 0.0).astype(BF16)
    send_x = mm(pick, tok_q[:, :width]).astype(BF16).reshape(chips, 4 * CAP, width)
    send_s = mm(pick_g.reshape(slots, 4 * tok), grad_q[:, :width]).astype(BF16)
    x, s = alone(ids, send_x, send_s.reshape(chips, 4 * CAP, width))
    x, s, (before, after), far = lax.optimization_barrier((x, s, near, far))
    x, s = x.reshape(slots, width), s.reshape(slots, width)
    weight = (shard, after, *far, before)

    starts = (2 * zh + jnp.arange(8, dtype=jnp.int32)) % 8 * piece
    expert = 2 * (4 * 2 * lax.axis_index("x") + 2 * lax.axis_index("y") + zl) + core
    starts = jnp.concatenate([starts, expert.astype(jnp.int32).reshape(1)])
    of = jax.ShapeDtypeStruct
    grads = tuple((piece * n, 3 * hid) for n in (2, 1, 2, 2, 1))
    pre_grad, spread, g_own, g_next, g_up, g_down, g_prev = call(
        forward_kernel,
        (of((slots, 2 * hid), BF16), of((slots, 2 * EXPERTS), F32))
        + tuple(of(shape, BF16) for shape in grads),
        (pl.ANY, pltpu.VMEM) + (pl.ANY,) * 5,
        [pltpu.VMEM((slots, hid), BF16), pltpu.VMEM((slots, 2 * hid), BF16)]
        + [pltpu.VMEM(shape, BF16) for shape in grads]
        + [pltpu.SemaphoreType.DMA((6,))],
        starts,
        x,
        s,
        *weight,
    )
    got_up, got_down = both_ways(g_up, g_down)

    wide = width + 2 * EXPERTS
    (back,) = call(
        back_kernel, (of((slots, wide), BF16),), (pltpu.VMEM,), [], starts, spread, pre_grad, *weight
    )
    (back,) = alone(ids, back.reshape(chips, 4 * CAP, wide))
    back, got_up, got_down = lax.optimization_barrier((back, got_up, got_down))
    part = mm(pick, back.reshape(slots, wide), ((0,), (0,)))
    part = part[: 2 * tok] + lax.ppermute(part[2 * tok :].astype(BF16), "core", SWAP).astype(F32)
    other = lax.ppermute(part[tok:].astype(BF16), "zl", SWAP)
    up = (g_next.astype(F32) + got_up[piece:].astype(F32)).astype(BF16)
    down = (g_prev.astype(F32) + got_down[:piece].astype(F32)).astype(BF16)
    other, up, down = lax.optimization_barrier((other, up, down))
    last_up, last_down = both_ways(up, down)
    part = part[:tok] + other.astype(F32)

    taken = part[:, width : width + EXPERTS].T
    mean = jnp.sum(taken, axis=0, keepdims=True)
    dlogits = jnp.where(chosen, (taken - gate * mean) * (1.0 - sig), 0.0).astype(BF16)
    term = mm(dlogits, tokens).astype(BF16).reshape(chips, 4, width)
    grad_tokens = (part[:, :width] + mm(dlogits, router, ((0,), (1,)))).astype(BF16)
    term = jnp.sum(a2a(term, PLANE).astype(F32), axis=0)
    term = term.reshape(2, 2, 8, width // 8).transpose(2, 0, 1, 3).reshape(chips, 2, width // 8)
    grad_router = jnp.sum(a2a(term, ("zh", "core", "zl")), axis=0)

    low = g_own[:piece].astype(F32) + last_up.astype(F32) + got_down[piece:].astype(F32)
    high = g_own[piece:].astype(F32) + got_up[:piece].astype(F32) + last_down.astype(F32)
    total = a2a(jnp.stack([low, high]).astype(BF16).reshape(2, piece, 3 * hid), "core")
    return (
        grad_tokens,
        total[:, :, :hid],
        total[:, :, hid : 2 * hid],
        jnp.swapaxes(total[:, :, 2 * hid :], 1, 2),
        grad_router,
    )


def solution(mesh):
    grid = Mesh(mesh.devices.reshape(4, 2, 4, 4, 2), AXES)
    dp, ex = ("zh", "core"), ("x", "y", "zl")
    rows = P(AXES, None)
    return jax.shard_map(
        per_device,
        mesh=grid,
        in_specs=(rows,) * 5 + (P(), P(ex, dp, None), P(ex, dp, None), P(ex, None, dp)),
        out_specs=(rows, P(ex, dp, None), P(ex, dp, None), P(ex, None, dp), P(ex, dp)),
        check_vma=False,
    )
```

```python
import jax
import jax.numpy as jnp
from jax import lax
from jax.experimental import pallas as pl
from jax.experimental.pallas import tpu as pltpu
from jax.sharding import Mesh
from jax.sharding import PartitionSpec as P

F32, BF16 = jnp.float32, jnp.bfloat16
AXES = ("zh", "core", "x", "y", "zl")
PLANE = ("x", "y")
CAP = 10
EXPERTS = 64
PLUS = [(i, (i + 1) % 4) for i in range(4)]
MINUS = [(i, (i + 3) % 4) for i in range(4)]
SWAP = [(0, 1), (1, 0)]


def mm(a, b, dims=((1,), (0,))):
    return lax.dot_general(a, b, (dims, ((), ())), preferred_element_type=F32)


def both_ways(up, down):
    return lax.ppermute(up, "zh", PLUS), lax.ppermute(down, "zh", MINUS)


def a2a(a, axes):
    return lax.all_to_all(a, axes, split_axis=0, concat_axis=0, tiled=True)


def alone(ids, *arrays):
    return lax.cond(
        ids[0, 0] >= 0, lambda *v: tuple(a2a(w, PLANE) for w in v), lambda *v: v, *arrays
    )


def at_unit(starts, unit, size):
    return pl.ds(pl.multiple_of(starts[unit], 256), size)


def forward_kernel(starts, x, s, own, after, far_lo, far_hi, prev, *refs):
    pre_out, spread, *outs = refs[:7]
    hidden, pre_grad, *grads, sems = refs[7:]
    hid = own.shape[1] // 3
    rows = x.shape[0] // 2
    pieces = ((own, 0), (after, 2), (far_lo, 4), (far_hi, 5), (prev, 6))

    @pl.loop(0, 2)
    def _(i):
        tile = pl.ds(pl.multiple_of(i * rows, rows), rows)
        pre = jnp.zeros((rows, 2 * hid), F32)
        for w, u in pieces:
            pre += mm(x[tile, at_unit(starts, u, w.shape[0])], w[:, : 2 * hid])
        hgrad = jnp.zeros((rows, hid), F32)
        for w, u in pieces:
            hgrad += mm(s[tile, at_unit(starts, u, w.shape[0])], w[:, 2 * hid :])
        gate_pre, up_pre = pre[:, :hid], pre[:, hid:]
        sg = jax.nn.sigmoid(gate_pre)
        act = gate_pre * sg
        h = (act * up_pre).astype(BF16)
        hidden[tile, :] = h
        share = jnp.sum(h.astype(F32) * hgrad, axis=1, keepdims=True)
        column = lax.broadcasted_iota(jnp.int32, (rows, spread.shape[1]), 1)
        spread[tile, :] = jnp.where(column == starts[8], share, 0.0)
        slope = sg * (1.0 + gate_pre * (1.0 - sg))
        pre_grad[tile, :hid] = (hgrad * up_pre * slope).astype(BF16)
        pre_grad[tile, hid:] = (hgrad * act).astype(BF16)

    copies = [pltpu.make_async_copy(pre_grad, pre_out, sems.at[len(outs)])]
    copies[0].start()
    firsts = (0, 2, 3, 5, 7)
    for k in (2, 3, 1, 4, 0):
        g = grads[k]
        for r in range(0, g.shape[0], 256):
            cols = at_unit(starts, firsts[k] + r // 256, 256)
            g[r : r + 256, : 2 * hid] = mm(x[:, cols], pre_grad[...], ((0,), (0,))).astype(BF16)
            g[r : r + 256, 2 * hid :] = mm(s[:, cols], hidden[...], ((0,), (0,))).astype(BF16)
        copies.append(pltpu.make_async_copy(g, outs[k], sems.at[k]))
        copies[-1].start()
    for copy in copies:
        copy.wait()


def back_kernel(starts, spread, pre_grad, own, after, far_lo, far_hi, prev, back):
    hid = own.shape[1] // 3
    rows = pre_grad.shape[0] // 2

    @pl.loop(0, 2)
    def _(i):
        tile = pl.ds(pl.multiple_of(i * rows, rows), rows)
        for w, u in ((own, 0), (after, 2), (far_lo, 4), (far_hi, 5), (prev, 6)):
            grad = mm(pre_grad[tile, :], w[:, : 2 * hid], ((1,), (1,)))
            back[tile, at_unit(starts, u, w.shape[0])] = grad.astype(BF16)
        back[tile, back.shape[1] - spread.shape[1] :] = spread[tile, :].astype(BF16)


def call(kernel, outs, spaces, scratch, *args):
    vmem = pl.BlockSpec(memory_space=pltpu.VMEM)
    smem = pl.BlockSpec(memory_space=pltpu.SMEM)
    return pl.pallas_call(
        kernel,
        out_shape=outs,
        in_specs=[smem if a.dtype == jnp.int32 else vmem for a in args],
        out_specs=[pl.BlockSpec(memory_space=space) for space in spaces],
        scratch_shapes=scratch,
        compiler_params=pltpu.CompilerParams(vmem_limit_bytes=40 * 2**20),
    )(*args)


def per_device(tokens, out_grad, ids, pos, keep, router, w_gate, w_up, w_down):
    tok, width = tokens.shape
    hid = w_gate.shape[2]
    piece = w_gate.shape[1]
    zh, core, zl = (lax.axis_index(n) for n in ("zh", "core", "zl"))
    chips = 16
    slots = chips * 4 * CAP

    experts = jnp.arange(EXPERTS, dtype=jnp.int32)
    hit = ids.T[None] == experts[:, None, None]
    chosen = jnp.any(hit, axis=1)
    held = hit & (keep.T > 0)[None]
    slot_t = (jnp.sum(jnp.where(held, pos.T[None] + 1, 0), axis=1) - 1).astype(BF16)
    logits = mm(router, tokens, ((0,), (1,)))
    sig = jax.nn.sigmoid(logits)
    prob = jnp.where(chosen, sig, 0.0)
    gate = prob / jnp.sum(prob, axis=0, keepdims=True)

    last = 2 * zl + core
    slot_c, gate_c = slot_t.T, gate.astype(BF16).T
    tok_e = jnp.concatenate([tokens, slot_c, jnp.zeros_like(gate_c)], axis=1)
    grad_e = jnp.concatenate([out_grad, slot_c, gate_c], axis=1)
    tok_z, grad_z = (lax.ppermute(v, "zl", SWAP) for v in (tok_e, grad_e))
    shard = a2a(jnp.concatenate([w_gate, w_up, jnp.swapaxes(w_down, 1, 2)], axis=2), "core")
    shard, tok_z, grad_z = lax.optimization_barrier((shard, tok_z, grad_z))
    shard = shard.reshape(2 * piece, 3 * hid)
    near = both_ways(shard, shard)

    def four(own, other):
        pair = jnp.concatenate([own, other], axis=0)
        return jnp.concatenate([pair, lax.ppermute(pair, "core", SWAP)], axis=0)

    every = 4 * jnp.arange(chips, dtype=jnp.int32) + last
    one = jnp.where(every[:, None] == experts[None, :], 1.0, 0.0).astype(BF16)

    def table(rows, at):
        return mm(one, rows[:, width + at : width + at + EXPERTS], ((1,), (1,)))

    place = jnp.arange(4 * CAP, dtype=jnp.int32)
    block = jnp.arange(4 * tok, dtype=jnp.int32) // tok
    same_block = (place // CAP)[:, None] == block[None, :]
    wanted = (place % CAP).astype(F32)[None, :, None]

    tok_q = four(tok_e, tok_z)
    grad_q = four(grad_e, grad_z)
    match = (table(tok_q, 0)[:, None, :] == wanted) & same_block
    pick = jnp.where(match, 1.0, 0.0).astype(BF16).reshape(slots, 4 * tok)
    pick_g = jnp.where(match, table(grad_q, EXPERTS)[:, None, :], 0.0).astype(BF16)
    send_x = mm(pick, tok_q[:, :width]).astype(BF16).reshape(chips, 4 * CAP, width)
    send_s = mm(pick_g.reshape(slots, 4 * tok), grad_q[:, :width]).astype(BF16)
    send_x, send_s = lax.optimization_barrier((send_x, send_s))
    (x,) = alone(ids, send_x)
    x, send_s, (before, after) = lax.optimization_barrier((x, send_s, near))
    halves = lax.optimization_barrier((before[:piece], after[piece:], send_s))
    far = both_ways(*halves[:2])
    (s,) = alone(ids, halves[2].reshape(chips, 4 * CAP, width))
    s, far = lax.optimization_barrier((s, far))
    x, s = x.reshape(slots, width), s.reshape(slots, width)
    weight = (shard, after, *far, before)

    starts = (2 * zh + jnp.arange(8, dtype=jnp.int32)) % 8 * piece
    expert = 2 * (4 * 2 * lax.axis_index("x") + 2 * lax.axis_index("y") + zl) + core
    starts = jnp.concatenate([starts, expert.astype(jnp.int32).reshape(1)])
    of = jax.ShapeDtypeStruct
    grads = tuple((piece * n, 3 * hid) for n in (2, 1, 2, 2, 1))
    pre_grad, spread, g_own, g_next, g_up, g_down, g_prev = call(
        forward_kernel,
        (of((slots, 2 * hid), BF16), of((slots, 2 * EXPERTS), F32))
        + tuple(of(shape, BF16) for shape in grads),
        (pl.ANY, pltpu.VMEM) + (pl.ANY,) * 5,
        [pltpu.VMEM((slots, hid), BF16), pltpu.VMEM((slots, 2 * hid), BF16)]
        + [pltpu.VMEM(shape, BF16) for shape in grads]
        + [pltpu.SemaphoreType.DMA((6,))],
        starts,
        x,
        s,
        *weight,
    )
    got_up, got_down = both_ways(g_up, g_down)

    wide = width + 2 * EXPERTS
    (back,) = call(
        back_kernel, (of((slots, wide), BF16),), (pltpu.VMEM,), [], starts, spread, pre_grad, *weight
    )
    (back,) = alone(ids, back.reshape(chips, 4 * CAP, wide))
    back, got_up, got_down = lax.optimization_barrier((back, got_up, got_down))
    part = mm(pick, back.reshape(slots, wide), ((0,), (0,)))
    part = part[: 2 * tok] + lax.ppermute(part[2 * tok :].astype(BF16), "core", SWAP).astype(F32)
    for_other = part[tok:].astype(BF16)
    up = (g_next.astype(F32) + got_up[piece:].astype(F32)).astype(BF16)
    down = (g_prev.astype(F32) + got_down[:piece].astype(F32)).astype(BF16)
    for_other, up, down = lax.optimization_barrier((for_other, up, down))
    other = lax.ppermute(for_other, "zl", SWAP)
    last_up, last_down = both_ways(up, down)
    part = part[:tok] + other.astype(F32)

    taken = part[:, width : width + EXPERTS].T
    mean = jnp.sum(taken, axis=0, keepdims=True)
    dlogits = jnp.where(chosen, (taken - gate * mean) * (1.0 - sig), 0.0).astype(BF16)
    term = mm(dlogits, tokens).astype(BF16).reshape(chips, 4, width)
    grad_tokens = (part[:, :width] + mm(dlogits, router, ((0,), (1,)))).astype(BF16)
    term = jnp.sum(a2a(term, PLANE).astype(F32), axis=0)
    term = term.reshape(2, 2, 8, width // 8).transpose(2, 0, 1, 3).reshape(chips, 2, width // 8)
    term, last_up, last_down = lax.optimization_barrier((term, last_up, last_down))
    term = a2a(term, ("zh", "core", "zl"))

    low = g_own[:piece].astype(F32) + last_up.astype(F32) + got_down[piece:].astype(F32)
    high = g_own[piece:].astype(F32) + got_up[:piece].astype(F32) + last_down.astype(F32)
    low, high = low.astype(BF16), high.astype(BF16)
    other = lax.ppermute(jnp.where(core == 0, high, low), "core", SWAP)
    mine = jnp.where(core == 0, low, high)
    total = jnp.stack([jnp.where(core == 0, mine, other), jnp.where(core == 0, other, mine)])
    total, term = lax.optimization_barrier((total, term))
    grad_router = jnp.sum(term, axis=0)
    return (
        grad_tokens,
        total[:, :, :hid],
        total[:, :, hid : 2 * hid],
        jnp.swapaxes(total[:, :, 2 * hid :], 1, 2),
        grad_router,
    )


def solution(mesh):
    grid = Mesh(mesh.devices.reshape(4, 2, 4, 4, 2), AXES)
    dp, ex = ("zh", "core"), ("x", "y", "zl")
    rows = P(AXES, None)
    return jax.shard_map(
        per_device,
        mesh=grid,
        in_specs=(rows,) * 5 + (P(), P(ex, dp, None), P(ex, dp, None), P(ex, None, dp)),
        out_specs=(rows, P(ex, dp, None), P(ex, dp, None), P(ex, None, dp), P(ex, dp)),
        check_vma=False,
    )
```

```python
import jax
import jax.numpy as jnp
from jax import lax
from jax.experimental import pallas as pl
from jax.experimental.pallas import tpu as pltpu
from jax.sharding import Mesh
from jax.sharding import PartitionSpec as P

F32, BF16 = jnp.float32, jnp.bfloat16
AXES = ("zh", "core", "x", "y", "zl")
PLANE = ("x", "y")
CAP = 10
EXPERTS = 64
PLUS = [(i, (i + 1) % 4) for i in range(4)]
MINUS = [(i, (i + 3) % 4) for i in range(4)]
SWAP = [(0, 1), (1, 0)]


def mm(a, b, dims=((1,), (0,))):
    return lax.dot_general(a, b, (dims, ((), ())), preferred_element_type=F32)


def both_ways(up, down):
    return lax.ppermute(up, "zh", PLUS), lax.ppermute(down, "zh", MINUS)


def a2a(a, axes):
    return lax.all_to_all(a, axes, split_axis=0, concat_axis=0, tiled=True)


def alone(ids, *arrays):
    return lax.cond(
        ids[0, 0] >= 0, lambda *v: tuple(a2a(w, PLANE) for w in v), lambda *v: v, *arrays
    )


def at_unit(starts, unit, size):
    return pl.ds(pl.multiple_of(starts[unit], 256), size)


def forward_kernel(starts, x, s, own, after, far_lo, far_hi, prev, *refs):
    pre_out, spread, *outs = refs[:7]
    hidden, pre_grad, *grads, sems = refs[7:]
    hid = own.shape[1] // 3
    rows = x.shape[0] // 2
    pieces = ((own, 0), (after, 2), (far_lo, 4), (far_hi, 5), (prev, 6))

    @pl.loop(0, 2)
    def _(i):
        tile = pl.ds(pl.multiple_of(i * rows, rows), rows)
        pre = jnp.zeros((rows, 2 * hid), F32)
        for w, u in pieces:
            pre += mm(x[tile, at_unit(starts, u, w.shape[0])], w[:, : 2 * hid])
        hgrad = jnp.zeros((rows, hid), F32)
        for w, u in pieces:
            hgrad += mm(s[tile, at_unit(starts, u, w.shape[0])], w[:, 2 * hid :])
        gate_pre, up_pre = pre[:, :hid], pre[:, hid:]
        sg = jax.nn.sigmoid(gate_pre)
        act = gate_pre * sg
        h = (act * up_pre).astype(BF16)
        hidden[tile, :] = h
        share = jnp.sum(h.astype(F32) * hgrad, axis=1, keepdims=True)
        column = lax.broadcasted_iota(jnp.int32, (rows, spread.shape[1]), 1)
        spread[tile, :] = jnp.where(column == starts[8], share, 0.0)
        slope = sg * (1.0 + gate_pre * (1.0 - sg))
        pre_grad[tile, :hid] = (hgrad * up_pre * slope).astype(BF16)
        pre_grad[tile, hid:] = (hgrad * act).astype(BF16)

    copies = [pltpu.make_async_copy(pre_grad, pre_out, sems.at[len(outs)])]
    copies[0].start()
    firsts = (0, 2, 3, 5, 7)
    for k in (2, 3, 1, 4, 0):
        g = grads[k]
        for r in range(0, g.shape[0], 256):
            cols = at_unit(starts, firsts[k] + r // 256, 256)
            g[r : r + 256, : 2 * hid] = mm(x[:, cols], pre_grad[...], ((0,), (0,))).astype(BF16)
            g[r : r + 256, 2 * hid :] = mm(s[:, cols], hidden[...], ((0,), (0,))).astype(BF16)
        copies.append(pltpu.make_async_copy(g, outs[k], sems.at[k]))
        copies[-1].start()
    for copy in copies:
        copy.wait()


def back_kernel(starts, spread, pre_grad, own, after, far_lo, far_hi, prev, back):
    hid = own.shape[1] // 3
    rows = pre_grad.shape[0] // 2

    @pl.loop(0, 2)
    def _(i):
        tile = pl.ds(pl.multiple_of(i * rows, rows), rows)
        for w, u in ((own, 0), (after, 2), (far_lo, 4), (far_hi, 5), (prev, 6)):
            grad = mm(pre_grad[tile, :], w[:, : 2 * hid], ((1,), (1,)))
            back[tile, at_unit(starts, u, w.shape[0])] = grad.astype(BF16)
        back[tile, back.shape[1] - spread.shape[1] :] = spread[tile, :].astype(BF16)


def call(kernel, outs, spaces, scratch, *args):
    vmem = pl.BlockSpec(memory_space=pltpu.VMEM)
    smem = pl.BlockSpec(memory_space=pltpu.SMEM)
    return pl.pallas_call(
        kernel,
        out_shape=outs,
        in_specs=[smem if a.dtype == jnp.int32 else vmem for a in args],
        out_specs=[pl.BlockSpec(memory_space=space) for space in spaces],
        scratch_shapes=scratch,
        compiler_params=pltpu.CompilerParams(vmem_limit_bytes=40 * 2**20),
    )(*args)


def per_device(tokens, out_grad, ids, pos, keep, router, w_gate, w_up, w_down):
    tok, width = tokens.shape
    hid = w_gate.shape[2]
    piece = w_gate.shape[1]
    zh, core, zl = (lax.axis_index(n) for n in ("zh", "core", "zl"))
    chips = 16
    slots = chips * 4 * CAP

    experts = jnp.arange(EXPERTS, dtype=jnp.int32)
    hit = ids.T[None] == experts[:, None, None]
    chosen = jnp.any(hit, axis=1)
    held = hit & (keep.T > 0)[None]
    slot_t = (jnp.sum(jnp.where(held, pos.T[None] + 1, 0), axis=1) - 1).astype(BF16)
    logits = mm(router, tokens, ((0,), (1,)))
    sig = jax.nn.sigmoid(logits)
    prob = jnp.where(chosen, sig, 0.0)
    gate = prob / jnp.sum(prob, axis=0, keepdims=True)

    last = 2 * zl + core
    slot_c, gate_c = slot_t.T, gate.astype(BF16).T
    tok_e = jnp.concatenate([tokens, slot_c, jnp.zeros_like(gate_c)], axis=1)
    grad_e = jnp.concatenate([out_grad, slot_c, gate_c], axis=1)
    tok_z, grad_z = (lax.ppermute(v, "zl", SWAP) for v in (tok_e, grad_e))
    shard = a2a(jnp.concatenate([w_gate, w_up, jnp.swapaxes(w_down, 1, 2)], axis=2), "core")
    shard, tok_z, grad_z = lax.optimization_barrier((shard, tok_z, grad_z))
    shard = shard.reshape(2 * piece, 3 * hid)
    near = both_ways(shard, shard)

    def four(own, other):
        pair = jnp.concatenate([own, other], axis=0)
        return jnp.concatenate([pair, lax.ppermute(pair, "core", SWAP)], axis=0)

    every = 4 * jnp.arange(chips, dtype=jnp.int32) + last
    one = jnp.where(every[:, None] == experts[None, :], 1.0, 0.0).astype(BF16)

    def table(rows, at):
        return mm(one, rows[:, width + at : width + at + EXPERTS], ((1,), (1,)))

    place = jnp.arange(4 * CAP, dtype=jnp.int32)
    block = jnp.arange(4 * tok, dtype=jnp.int32) // tok
    same_block = (place // CAP)[:, None] == block[None, :]
    wanted = (place % CAP).astype(F32)[None, :, None]

    tok_q = four(tok_e, tok_z)
    grad_q = four(grad_e, grad_z)
    match = (table(tok_q, 0)[:, None, :] == wanted) & same_block
    pick = jnp.where(match, 1.0, 0.0).astype(BF16).reshape(slots, 4 * tok)
    pick_g = jnp.where(match, table(grad_q, EXPERTS)[:, None, :], 0.0).astype(BF16)
    send_x = mm(pick, tok_q[:, :width]).astype(BF16).reshape(chips, 4 * CAP, width)
    send_s = mm(pick_g.reshape(slots, 4 * tok), grad_q[:, :width]).astype(BF16)
    send_x, send_s = lax.optimization_barrier((send_x, send_s))
    (x,) = alone(ids, send_x)
    x, send_s, (before, after) = lax.optimization_barrier((x, send_s, near))
    halves = lax.optimization_barrier((before[:piece], after[piece:], send_s))
    far = both_ways(*halves[:2])
    (s,) = alone(ids, halves[2].reshape(chips, 4 * CAP, width))
    s, far = lax.optimization_barrier((s, far))
    x, s = x.reshape(slots, width), s.reshape(slots, width)
    weight = (shard, after, *far, before)

    starts = (2 * zh + jnp.arange(8, dtype=jnp.int32)) % 8 * piece
    expert = 2 * (4 * 2 * lax.axis_index("x") + 2 * lax.axis_index("y") + zl) + core
    starts = jnp.concatenate([starts, expert.astype(jnp.int32).reshape(1)])
    of = jax.ShapeDtypeStruct
    grads = tuple((piece * n, 3 * hid) for n in (2, 1, 2, 2, 1))
    pre_grad, spread, g_own, g_next, g_up, g_down, g_prev = call(
        forward_kernel,
        (of((slots, 2 * hid), BF16), of((slots, 2 * EXPERTS), F32))
        + tuple(of(shape, BF16) for shape in grads),
        (pl.ANY, pltpu.VMEM) + (pl.ANY,) * 5,
        [pltpu.VMEM((slots, hid), BF16), pltpu.VMEM((slots, 2 * hid), BF16)]
        + [pltpu.VMEM(shape, BF16) for shape in grads]
        + [pltpu.SemaphoreType.DMA((6,))],
        starts,
        x,
        s,
        *weight,
    )
    got_up, got_down = both_ways(g_up, g_down)

    wide = width + 2 * EXPERTS
    (back,) = call(
        back_kernel, (of((slots, wide), BF16),), (pltpu.VMEM,), [], starts, spread, pre_grad, *weight
    )
    (back,) = alone(ids, back.reshape(chips, 4 * CAP, wide))
    back, got_up, got_down = lax.optimization_barrier((back, got_up, got_down))
    back = back.reshape(slots, wide)
    taken = mm(pick, back[:, width:], ((0,), (0,)))
    taken = taken[: 2 * tok] + lax.ppermute(taken[2 * tok :].astype(BF16), "core", SWAP).astype(F32)
    other_taken = lax.ppermute(taken[tok:].astype(BF16), "zl", SWAP)
    part = mm(pick, back[:, :width], ((0,), (0,)))
    part = part[: 2 * tok] + lax.ppermute(part[2 * tok :].astype(BF16), "core", SWAP).astype(F32)
    for_other = part[tok:].astype(BF16)
    up = (g_next.astype(F32) + got_up[piece:].astype(F32)).astype(BF16)
    down = (g_prev.astype(F32) + got_down[:piece].astype(F32)).astype(BF16)
    for_other, up, down, other_taken = lax.optimization_barrier(
        (for_other, up, down, other_taken)
    )
    other = lax.ppermute(for_other, "zl", SWAP)
    last_up, last_down = both_ways(up, down)
    taken = (taken[:tok] + other_taken.astype(F32))[:, :EXPERTS].T
    mean = jnp.sum(taken, axis=0, keepdims=True)
    dlogits = jnp.where(chosen, (taken - gate * mean) * (1.0 - sig), 0.0).astype(BF16)
    term = mm(dlogits, tokens).astype(BF16).reshape(chips, 4, width)
    term = jnp.sum(a2a(term, PLANE).astype(F32), axis=0)
    term = term.reshape(2, 2, 8, width // 8).transpose(2, 0, 1, 3).reshape(chips, 2, width // 8)
    term, other, last_up, last_down = lax.optimization_barrier((term, other, last_up, last_down))
    term = a2a(term, ("zh", "core", "zl"))
    part = part[:tok] + other.astype(F32)
    grad_tokens = (part + mm(dlogits, router, ((0,), (1,)))).astype(BF16)

    low = g_own[:piece].astype(F32) + last_up.astype(F32) + got_down[piece:].astype(F32)
    high = g_own[piece:].astype(F32) + got_up[:piece].astype(F32) + last_down.astype(F32)
    low, high = low.astype(BF16), high.astype(BF16)
    other = lax.ppermute(jnp.where(core == 0, high, low), "core", SWAP)
    mine = jnp.where(core == 0, low, high)
    total = jnp.stack([jnp.where(core == 0, mine, other), jnp.where(core == 0, other, mine)])
    total, term = lax.optimization_barrier((total, term))
    grad_router = jnp.sum(term, axis=0)
    return (
        grad_tokens,
        total[:, :, :hid],
        total[:, :, hid : 2 * hid],
        jnp.swapaxes(total[:, :, 2 * hid :], 1, 2),
        grad_router,
    )


def solution(mesh):
    grid = Mesh(mesh.devices.reshape(4, 2, 4, 4, 2), AXES)
    dp, ex = ("zh", "core"), ("x", "y", "zl")
    rows = P(AXES, None)
    return jax.shard_map(
        per_device,
        mesh=grid,
        in_specs=(rows,) * 5 + (P(), P(ex, dp, None), P(ex, dp, None), P(ex, None, dp)),
        out_specs=(rows, P(ex, dp, None), P(ex, dp, None), P(ex, None, dp), P(ex, dp)),
        check_vma=False,
    )
```

```python
import jax
import jax.numpy as jnp
from jax import lax
from jax.experimental import pallas as pl
from jax.experimental.pallas import tpu as pltpu
from jax.sharding import Mesh
from jax.sharding import PartitionSpec as P

F32, BF16 = jnp.float32, jnp.bfloat16
AXES = ("zh", "core", "x", "y", "zl")
PLANE = ("x", "y")
CAP = 10
EXPERTS = 64
PLUS = [(i, (i + 1) % 4) for i in range(4)]
MINUS = [(i, (i + 3) % 4) for i in range(4)]
SWAP = [(0, 1), (1, 0)]


def mm(a, b, dims=((1,), (0,))):
    return lax.dot_general(a, b, (dims, ((), ())), preferred_element_type=F32)


def both_ways(up, down):
    return lax.ppermute(up, "zh", PLUS), lax.ppermute(down, "zh", MINUS)


def a2a(a, axes):
    return lax.all_to_all(a, axes, split_axis=0, concat_axis=0, tiled=True)


def alone(ids, *arrays):
    return lax.cond(
        ids[0, 0] >= 0, lambda *v: tuple(a2a(w, PLANE) for w in v), lambda *v: v, *arrays
    )


def at_unit(starts, unit, size):
    return pl.ds(pl.multiple_of(starts[unit], 256), size)


def forward_kernel(starts, x, s, own, after, far_lo, far_hi, prev, *refs):
    pre_out, spread, *outs = refs[:7]
    hidden, pre_grad, *grads, sems = refs[7:]
    hid = own.shape[1] // 3
    rows = x.shape[0] // 2
    pieces = ((own, 0), (after, 2), (far_lo, 4), (far_hi, 5), (prev, 6))

    @pl.loop(0, 2)
    def _(i):
        tile = pl.ds(pl.multiple_of(i * rows, rows), rows)
        pre = jnp.zeros((rows, 2 * hid), F32)
        for w, u in pieces:
            pre += mm(x[tile, at_unit(starts, u, w.shape[0])], w[:, : 2 * hid])
        hgrad = jnp.zeros((rows, hid), F32)
        for w, u in pieces:
            hgrad += mm(s[tile, at_unit(starts, u, w.shape[0])], w[:, 2 * hid :])
        gate_pre, up_pre = pre[:, :hid], pre[:, hid:]
        sg = jax.nn.sigmoid(gate_pre)
        act = gate_pre * sg
        h = (act * up_pre).astype(BF16)
        hidden[tile, :] = h
        share = jnp.sum(h.astype(F32) * hgrad, axis=1, keepdims=True)
        column = lax.broadcasted_iota(jnp.int32, (rows, spread.shape[1]), 1)
        spread[tile, :] = jnp.where(column == starts[8], share, 0.0)
        slope = sg * (1.0 + gate_pre * (1.0 - sg))
        pre_grad[tile, :hid] = (hgrad * up_pre * slope).astype(BF16)
        pre_grad[tile, hid:] = (hgrad * act).astype(BF16)

    copies = [pltpu.make_async_copy(pre_grad, pre_out, sems.at[len(outs)])]
    copies[0].start()
    firsts = (0, 2, 3, 5, 7)
    for k in (2, 3, 1, 4, 0):
        g = grads[k]
        for r in range(0, g.shape[0], 256):
            cols = at_unit(starts, firsts[k] + r // 256, 256)
            g[r : r + 256, : 2 * hid] = mm(x[:, cols], pre_grad[...], ((0,), (0,))).astype(BF16)
            g[r : r + 256, 2 * hid :] = mm(s[:, cols], hidden[...], ((0,), (0,))).astype(BF16)
        copies.append(pltpu.make_async_copy(g, outs[k], sems.at[k]))
        copies[-1].start()
    for copy in copies:
        copy.wait()


def back_kernel(starts, spread, pre_grad, own, after, far_lo, far_hi, prev, back):
    hid = own.shape[1] // 3
    rows = pre_grad.shape[0] // 2

    @pl.loop(0, 2)
    def _(i):
        tile = pl.ds(pl.multiple_of(i * rows, rows), rows)
        for w, u in ((own, 0), (after, 2), (far_lo, 4), (far_hi, 5), (prev, 6)):
            grad = mm(pre_grad[tile, :], w[:, : 2 * hid], ((1,), (1,)))
            back[tile, at_unit(starts, u, w.shape[0])] = grad.astype(BF16)
        back[tile, back.shape[1] - spread.shape[1] :] = spread[tile, :].astype(BF16)


def call(kernel, outs, spaces, scratch, *args):
    vmem = pl.BlockSpec(memory_space=pltpu.VMEM)
    smem = pl.BlockSpec(memory_space=pltpu.SMEM)
    return pl.pallas_call(
        kernel,
        out_shape=outs,
        in_specs=[smem if a.dtype == jnp.int32 else vmem for a in args],
        out_specs=[pl.BlockSpec(memory_space=space) for space in spaces],
        scratch_shapes=scratch,
        compiler_params=pltpu.CompilerParams(vmem_limit_bytes=40 * 2**20),
    )(*args)


def per_device(tokens, out_grad, ids, pos, keep, router, w_gate, w_up, w_down):
    tok, width = tokens.shape
    hid = w_gate.shape[2]
    piece = w_gate.shape[1]
    zh, core, zl = (lax.axis_index(n) for n in ("zh", "core", "zl"))
    chips = 16
    slots = chips * 4 * CAP

    experts = jnp.arange(EXPERTS, dtype=jnp.int32)
    hit = ids.T[None] == experts[:, None, None]
    chosen = jnp.any(hit, axis=1)
    held = hit & (keep.T > 0)[None]
    slot_t = (jnp.sum(jnp.where(held, pos.T[None] + 1, 0), axis=1) - 1).astype(BF16)
    logits = mm(router, tokens, ((0,), (1,)))
    sig = jax.nn.sigmoid(logits)
    prob = jnp.where(chosen, sig, 0.0)
    gate = prob / jnp.sum(prob, axis=0, keepdims=True)

    last = 2 * zl + core
    slot_c, gate_c = slot_t.T, gate.astype(BF16).T
    tok_e = jnp.concatenate([tokens, slot_c, jnp.zeros_like(gate_c)], axis=1)
    grad_e = jnp.concatenate([out_grad, slot_c, gate_c], axis=1)
    tok_z, grad_z = (lax.ppermute(v, "zl", SWAP) for v in (tok_e, grad_e))
    shard = a2a(jnp.concatenate([w_gate, w_up, jnp.swapaxes(w_down, 1, 2)], axis=2), "core")
    shard, tok_z, grad_z = lax.optimization_barrier((shard, tok_z, grad_z))
    shard = shard.reshape(2 * piece, 3 * hid)
    near = both_ways(shard, shard)

    def four(own, other):
        pair = jnp.concatenate([own, other], axis=0)
        return jnp.concatenate([pair, lax.ppermute(pair, "core", SWAP)], axis=0)

    every = 4 * jnp.arange(chips, dtype=jnp.int32) + last
    one = jnp.where(every[:, None] == experts[None, :], 1.0, 0.0).astype(BF16)

    def table(rows, at):
        return mm(one, rows[:, width + at : width + at + EXPERTS], ((1,), (1,)))

    place = jnp.arange(4 * CAP, dtype=jnp.int32)
    block = jnp.arange(4 * tok, dtype=jnp.int32) // tok
    same_block = (place // CAP)[:, None] == block[None, :]
    wanted = (place % CAP).astype(F32)[None, :, None]

    tok_q = four(tok_e, tok_z)
    grad_q = four(grad_e, grad_z)
    match = (table(tok_q, 0)[:, None, :] == wanted) & same_block
    pick = jnp.where(match, 1.0, 0.0).astype(BF16).reshape(slots, 4 * tok)
    pick_g = jnp.where(match, table(grad_q, EXPERTS)[:, None, :], 0.0).astype(BF16)
    send_x = mm(pick, tok_q[:, :width]).astype(BF16).reshape(chips, 4 * CAP, width)
    send_s = mm(pick_g.reshape(slots, 4 * tok), grad_q[:, :width]).astype(BF16)
    send_x, send_s = lax.optimization_barrier((send_x, send_s))
    (x,) = alone(ids, send_x)
    x, send_s, (before, after) = lax.optimization_barrier((x, send_s, near))
    halves = lax.optimization_barrier((before[:piece], after[piece:], send_s))
    far = both_ways(*halves[:2])
    (s,) = alone(ids, halves[2].reshape(chips, 4 * CAP, width))
    s, far = lax.optimization_barrier((s, far))
    x, s = x.reshape(slots, width), s.reshape(slots, width)
    weight = (shard, after, *far, before)

    starts = (2 * zh + jnp.arange(8, dtype=jnp.int32)) % 8 * piece
    expert = 2 * (4 * 2 * lax.axis_index("x") + 2 * lax.axis_index("y") + zl) + core
    starts = jnp.concatenate([starts, expert.astype(jnp.int32).reshape(1)])
    of = jax.ShapeDtypeStruct
    grads = tuple((piece * n, 3 * hid) for n in (2, 1, 2, 2, 1))
    pre_grad, spread, g_own, g_next, g_up, g_down, g_prev = call(
        forward_kernel,
        (of((slots, 2 * hid), BF16), of((slots, 2 * EXPERTS), F32))
        + tuple(of(shape, BF16) for shape in grads),
        (pl.ANY, pltpu.VMEM) + (pl.ANY,) * 5,
        [pltpu.VMEM((slots, hid), BF16), pltpu.VMEM((slots, 2 * hid), BF16)]
        + [pltpu.VMEM(shape, BF16) for shape in grads]
        + [pltpu.SemaphoreType.DMA((6,))],
        starts,
        x,
        s,
        *weight,
    )
    got_up, got_down = both_ways(g_up, g_down)

    wide = width + 2 * EXPERTS
    (back,) = call(
        back_kernel, (of((slots, wide), BF16),), (pltpu.VMEM,), [], starts, spread, pre_grad, *weight
    )
    (back,) = alone(ids, back.reshape(chips, 4 * CAP, wide))
    back, got_up, got_down = lax.optimization_barrier((back, got_up, got_down))
    back = back.reshape(slots, wide)
    taken = mm(pick, back[:, width:], ((0,), (0,)))
    taken = taken[: 2 * tok] + lax.ppermute(taken[2 * tok :].astype(BF16), "core", SWAP).astype(F32)
    other_taken = lax.ppermute(taken[tok:].astype(BF16), "zl", SWAP)
    part = mm(pick, back[:, :width], ((0,), (0,)))
    part = part[: 2 * tok] + lax.ppermute(part[2 * tok :].astype(BF16), "core", SWAP).astype(F32)
    for_other = part[tok:].astype(BF16)
    up = (g_next.astype(F32) + got_up[piece:].astype(F32)).astype(BF16)
    down = (g_prev.astype(F32) + got_down[:piece].astype(F32)).astype(BF16)
    for_other, up, down, other_taken = lax.optimization_barrier(
        (for_other, up, down, other_taken)
    )
    other = lax.ppermute(for_other, "zl", SWAP)
    last_up, last_down = both_ways(up, down)
    taken = (taken[:tok] + other_taken.astype(F32))[:, :EXPERTS].T
    mean = jnp.sum(taken, axis=0, keepdims=True)
    dlogits = jnp.where(chosen, (taken - gate * mean) * (1.0 - sig), 0.0).astype(BF16)
    term = mm(dlogits, tokens).astype(BF16).reshape(chips, 4, width)
    term = jnp.sum(a2a(term, PLANE).astype(F32), axis=0)
    term = term.reshape(2, 2, 8, width // 8).transpose(2, 0, 1, 3).reshape(chips, 2, width // 8)
    term = a2a(term, ("zh", "core", "zl"))
    term, other, last_up, last_down = lax.optimization_barrier((term, other, last_up, last_down))
    part = part[:tok] + other.astype(F32)
    grad_tokens = (part + mm(dlogits, router, ((0,), (1,)))).astype(BF16)

    low = g_own[:piece].astype(F32) + last_up.astype(F32) + got_down[piece:].astype(F32)
    high = g_own[piece:].astype(F32) + got_up[:piece].astype(F32) + last_down.astype(F32)
    low, high = low.astype(BF16), high.astype(BF16)
    other = lax.ppermute(jnp.where(core == 0, high, low), "core", SWAP)
    mine = jnp.where(core == 0, low, high)
    grad_router = jnp.sum(term, axis=0)

    def by_expert(at):
        cols = slice(at * hid, (at + 1) * hid)
        a, b = mine[:, cols], other[:, cols]
        return jnp.stack([jnp.where(core == 0, a, b), jnp.where(core == 0, b, a)])

    return (
        grad_tokens,
        by_expert(0),
        by_expert(1),
        jnp.swapaxes(by_expert(2), 1, 2),
        grad_router,
    )


def solution(mesh):
    grid = Mesh(mesh.devices.reshape(4, 2, 4, 4, 2), AXES)
    dp, ex = ("zh", "core"), ("x", "y", "zl")
    rows = P(AXES, None)
    return jax.shard_map(
        per_device,
        mesh=grid,
        in_specs=(rows,) * 5 + (P(), P(ex, dp, None), P(ex, dp, None), P(ex, None, dp)),
        out_specs=(rows, P(ex, dp, None), P(ex, dp, None), P(ex, None, dp), P(ex, dp)),
        check_vma=False,
    )
```

```python
import jax
import jax.numpy as jnp
from jax import lax
from jax.experimental import pallas as pl
from jax.experimental.pallas import tpu as pltpu
from jax.sharding import Mesh
from jax.sharding import PartitionSpec as P

F32, BF16 = jnp.float32, jnp.bfloat16
AXES = ("zh", "core", "x", "y", "zl")
PLANE = ("x", "y")
CAP = 10
EXPERTS = 64
PLUS = [(i, (i + 1) % 4) for i in range(4)]
MINUS = [(i, (i + 3) % 4) for i in range(4)]
SWAP = [(0, 1), (1, 0)]


def mm(a, b, dims=((1,), (0,))):
    return lax.dot_general(a, b, (dims, ((), ())), preferred_element_type=F32)


def both_ways(up, down):
    return lax.ppermute(up, "zh", PLUS), lax.ppermute(down, "zh", MINUS)


def a2a(a, axes):
    return lax.all_to_all(a, axes, split_axis=0, concat_axis=0, tiled=True)


def alone(ids, *arrays):
    return lax.cond(
        ids[0, 0] >= 0, lambda *v: tuple(a2a(w, PLANE) for w in v), lambda *v: v, *arrays
    )


def at_unit(starts, unit, size):
    return pl.ds(pl.multiple_of(starts[unit], 256), size)


def forward_kernel(starts, x, s, own, after, far_lo, far_hi, prev, *refs):
    pre_out, spread, *outs = refs[:7]
    hidden, pre_grad, *grads, sems = refs[7:]
    hid = own.shape[1] // 3
    rows = x.shape[0]
    pieces = ((own, 0), (after, 2), (far_lo, 4), (far_hi, 5), (prev, 6))

    @pl.loop(0, 1)
    def _(i):
        tile = pl.ds(pl.multiple_of(i * rows, rows), rows)
        pre = jnp.zeros((rows, 2 * hid), F32)
        for w, u in pieces:
            pre += mm(x[tile, at_unit(starts, u, w.shape[0])], w[:, : 2 * hid])
        hgrad = jnp.zeros((rows, hid), F32)
        for w, u in pieces:
            hgrad += mm(s[tile, at_unit(starts, u, w.shape[0])], w[:, 2 * hid :])
        gate_pre, up_pre = pre[:, :hid], pre[:, hid:]
        sg = jax.nn.sigmoid(gate_pre)
        act = gate_pre * sg
        h = (act * up_pre).astype(BF16)
        hidden[tile, :] = h
        share = jnp.sum(h.astype(F32) * hgrad, axis=1, keepdims=True)
        column = lax.broadcasted_iota(jnp.int32, (rows, spread.shape[1]), 1)
        spread[tile, :] = jnp.where(column == starts[8], share, 0.0)
        slope = sg * (1.0 + gate_pre * (1.0 - sg))
        pre_grad[tile, :hid] = (hgrad * up_pre * slope).astype(BF16)
        pre_grad[tile, hid:] = (hgrad * act).astype(BF16)

    copies = [pltpu.make_async_copy(pre_grad, pre_out, sems.at[len(outs)])]
    copies[0].start()
    firsts = (0, 2, 3, 5, 7)
    for k in (2, 3, 1, 4, 0):
        g = grads[k]
        for r in range(0, g.shape[0], 256):
            cols = at_unit(starts, firsts[k] + r // 256, 256)
            g[r : r + 256, : 2 * hid] = mm(x[:, cols], pre_grad[...], ((0,), (0,))).astype(BF16)
            g[r : r + 256, 2 * hid :] = mm(s[:, cols], hidden[...], ((0,), (0,))).astype(BF16)
        copies.append(pltpu.make_async_copy(g, outs[k], sems.at[k]))
        copies[-1].start()
    for copy in copies:
        copy.wait()


def back_kernel(starts, spread, pre_grad, own, after, far_lo, far_hi, prev, back):
    hid = own.shape[1] // 3
    rows = pre_grad.shape[0]

    @pl.loop(0, 1)
    def _(i):
        tile = pl.ds(pl.multiple_of(i * rows, rows), rows)
        for w, u in ((own, 0), (after, 2), (far_lo, 4), (far_hi, 5), (prev, 6)):
            grad = mm(pre_grad[tile, :], w[:, : 2 * hid], ((1,), (1,)))
            back[tile, at_unit(starts, u, w.shape[0])] = grad.astype(BF16)
        back[tile, back.shape[1] - spread.shape[1] :] = spread[tile, :].astype(BF16)


def call(kernel, outs, spaces, scratch, *args):
    vmem = pl.BlockSpec(memory_space=pltpu.VMEM)
    smem = pl.BlockSpec(memory_space=pltpu.SMEM)
    return pl.pallas_call(
        kernel,
        out_shape=outs,
        in_specs=[smem if a.dtype == jnp.int32 else vmem for a in args],
        out_specs=[pl.BlockSpec(memory_space=space) for space in spaces],
        scratch_shapes=scratch,
        compiler_params=pltpu.CompilerParams(vmem_limit_bytes=40 * 2**20),
    )(*args)


def per_device(tokens, out_grad, ids, pos, keep, router, w_gate, w_up, w_down):
    tok, width = tokens.shape
    hid = w_gate.shape[2]
    piece = w_gate.shape[1]
    zh, core, zl = (lax.axis_index(n) for n in ("zh", "core", "zl"))
    chips = 16
    slots = chips * 4 * CAP

    experts = jnp.arange(EXPERTS, dtype=jnp.int32)
    hit = ids.T[None] == experts[:, None, None]
    chosen = jnp.any(hit, axis=1)
    held = hit & (keep.T > 0)[None]
    slot_t = (jnp.sum(jnp.where(held, pos.T[None] + 1, 0), axis=1) - 1).astype(BF16)
    logits = mm(router, tokens, ((0,), (1,)))
    sig = jax.nn.sigmoid(logits)
    prob = jnp.where(chosen, sig, 0.0)
    gate = prob / jnp.sum(prob, axis=0, keepdims=True)

    last = 2 * zl + core
    slot_c, gate_c = slot_t.T, gate.astype(BF16).T
    tok_e = jnp.concatenate([tokens, slot_c, jnp.zeros_like(gate_c)], axis=1)
    grad_e = jnp.concatenate([out_grad, slot_c, gate_c], axis=1)
    tok_z, grad_z = (lax.ppermute(v, "zl", SWAP) for v in (tok_e, grad_e))
    shard = a2a(jnp.concatenate([w_gate, w_up, jnp.swapaxes(w_down, 1, 2)], axis=2), "core")
    shard, tok_z, grad_z = lax.optimization_barrier((shard, tok_z, grad_z))
    shard = shard.reshape(2 * piece, 3 * hid)
    near = both_ways(shard, shard)

    def four(own, other):
        pair = jnp.concatenate([own, other], axis=0)
        return jnp.concatenate([pair, lax.ppermute(pair, "core", SWAP)], axis=0)

    every = 4 * jnp.arange(chips, dtype=jnp.int32) + last
    one = jnp.where(every[:, None] == experts[None, :], 1.0, 0.0).astype(BF16)

    def table(rows, at):
        return mm(one, rows[:, width + at : width + at + EXPERTS], ((1,), (1,)))

    place = jnp.arange(4 * CAP, dtype=jnp.int32)
    block = jnp.arange(4 * tok, dtype=jnp.int32) // tok
    same_block = (place // CAP)[:, None] == block[None, :]
    wanted = (place % CAP).astype(F32)[None, :, None]

    tok_q = four(tok_e, tok_z)
    grad_q = four(grad_e, grad_z)
    match = (table(tok_q, 0)[:, None, :] == wanted) & same_block
    pick = jnp.where(match, 1.0, 0.0).astype(BF16).reshape(slots, 4 * tok)
    pick_g = jnp.where(match, table(grad_q, EXPERTS)[:, None, :], 0.0).astype(BF16)
    send_x = mm(pick, tok_q[:, :width]).astype(BF16).reshape(chips, 4 * CAP, width)
    send_s = mm(pick_g.reshape(slots, 4 * tok), grad_q[:, :width]).astype(BF16)
    send_x, send_s = lax.optimization_barrier((send_x, send_s))
    (x,) = alone(ids, send_x)
    x, send_s, (before, after) = lax.optimization_barrier((x, send_s, near))
    halves = lax.optimization_barrier((before[:piece], after[piece:], send_s))
    far = both_ways(*halves[:2])
    (s,) = alone(ids, halves[2].reshape(chips, 4 * CAP, width))
    s, far = lax.optimization_barrier((s, far))
    x, s = x.reshape(slots, width), s.reshape(slots, width)
    weight = (shard, after, *far, before)

    starts = (2 * zh + jnp.arange(8, dtype=jnp.int32)) % 8 * piece
    expert = 2 * (4 * 2 * lax.axis_index("x") + 2 * lax.axis_index("y") + zl) + core
    starts = jnp.concatenate([starts, expert.astype(jnp.int32).reshape(1)])
    of = jax.ShapeDtypeStruct
    grads = tuple((piece * n, 3 * hid) for n in (2, 1, 2, 2, 1))
    pre_grad, spread, g_own, g_next, g_up, g_down, g_prev = call(
        forward_kernel,
        (of((slots, 2 * hid), BF16), of((slots, 2 * EXPERTS), F32))
        + tuple(of(shape, BF16) for shape in grads),
        (pl.ANY, pltpu.VMEM) + (pl.ANY,) * 5,
        [pltpu.VMEM((slots, hid), BF16), pltpu.VMEM((slots, 2 * hid), BF16)]
        + [pltpu.VMEM(shape, BF16) for shape in grads]
        + [pltpu.SemaphoreType.DMA((6,))],
        starts,
        x,
        s,
        *weight,
    )
    got_up, got_down = both_ways(g_up, g_down)

    wide = width + 2 * EXPERTS
    (back,) = call(
        back_kernel, (of((slots, wide), BF16),), (pltpu.VMEM,), [], starts, spread, pre_grad, *weight
    )
    (back,) = alone(ids, back.reshape(chips, 4 * CAP, wide))
    back, got_up, got_down = lax.optimization_barrier((back, got_up, got_down))
    back = back.reshape(slots, wide)
    taken = mm(pick, back[:, width:], ((0,), (0,)))
    taken = taken[: 2 * tok] + lax.ppermute(taken[2 * tok :].astype(BF16), "core", SWAP).astype(F32)
    other_taken = lax.ppermute(taken[tok:].astype(BF16), "zl", SWAP)
    part = mm(pick, back[:, :width], ((0,), (0,)))
    part = part[: 2 * tok] + lax.ppermute(part[2 * tok :].astype(BF16), "core", SWAP).astype(F32)
    for_other = part[tok:].astype(BF16)
    up = (g_next.astype(F32) + got_up[piece:].astype(F32)).astype(BF16)
    down = (g_prev.astype(F32) + got_down[:piece].astype(F32)).astype(BF16)
    for_other, up, down, other_taken = lax.optimization_barrier(
        (for_other, up, down, other_taken)
    )
    other = lax.ppermute(for_other, "zl", SWAP)
    last_up, last_down = both_ways(up, down)
    taken = (taken[:tok] + other_taken.astype(F32))[:, :EXPERTS].T
    mean = jnp.sum(taken, axis=0, keepdims=True)
    dlogits = jnp.where(chosen, (taken - gate * mean) * (1.0 - sig), 0.0).astype(BF16)
    term = mm(dlogits, tokens).astype(BF16).reshape(chips, 4, width)
    term = jnp.sum(a2a(term, PLANE).astype(F32), axis=0)
    term = term.reshape(2, 2, 8, width // 8).transpose(2, 0, 1, 3).reshape(chips, 2, width // 8)
    term = a2a(term, ("zh", "core", "zl"))
    term, other, last_up, last_down = lax.optimization_barrier((term, other, last_up, last_down))
    part = part[:tok] + other.astype(F32)
    grad_tokens = (part + mm(dlogits, router, ((0,), (1,)))).astype(BF16)

    low = g_own[:piece].astype(F32) + last_up.astype(F32) + got_down[piece:].astype(F32)
    high = g_own[piece:].astype(F32) + got_up[:piece].astype(F32) + last_down.astype(F32)
    low, high = low.astype(BF16), high.astype(BF16)
    other = lax.ppermute(jnp.where(core == 0, high, low), "core", SWAP)
    mine = jnp.where(core == 0, low, high)
    grad_router = jnp.sum(term, axis=0)

    def by_expert(at):
        cols = slice(at * hid, (at + 1) * hid)
        a, b = mine[:, cols], other[:, cols]
        return jnp.stack([jnp.where(core == 0, a, b), jnp.where(core == 0, b, a)])

    return (
        grad_tokens,
        by_expert(0),
        by_expert(1),
        jnp.swapaxes(by_expert(2), 1, 2),
        grad_router,
    )


def solution(mesh):
    grid = Mesh(mesh.devices.reshape(4, 2, 4, 4, 2), AXES)
    dp, ex = ("zh", "core"), ("x", "y", "zl")
    rows = P(AXES, None)
    return jax.shard_map(
        per_device,
        mesh=grid,
        in_specs=(rows,) * 5 + (P(), P(ex, dp, None), P(ex, dp, None), P(ex, None, dp)),
        out_specs=(rows, P(ex, dp, None), P(ex, dp, None), P(ex, None, dp), P(ex, dp)),
        check_vma=False,
    )
```
